768 devices in a mesh: occ: 8 (over x, core), vir: 96 (over y, z).
Axes of the slice: x: 4, y: 8, z: 12, core: 2. Of those that a mesh axis runs over, the one named last changes fastest.
Arguments:
- amplitudes: bfloat16 [4096, 3072], P('occ', 'vir'), may hold values from -6 to 6
- integrals: bfloat16 [3072, 98304], P('occ', 'vir'), may hold values from -0.109375 to 0.109375
- amp_mask: int32 [64, 48], P('occ'), may hold values 0 or 1
- int_mask: int32 [48, 1536], P('occ', 'vir'), may hold values 0 or 1
Outputs:
- ladder: bfloat16 [4096, 98304], P('occ', 'vir')
The draws below stay inside these ranges and needn't reach their ends.
All inputs are finite; a program needn't handle non-finite values. No bound on the sum of `amp_mask` or of `int_mask` on one device may be relied on, other than what follows from the above.
Results may differ from the reference program's by a relative error of at most 0.001.
Values may be sent and summed in bfloat16 or wider, within the bound.
No kernel may reach another device: no remote copies, remote signals or barrier semaphores. Data moves between devices by JAX's collectives and lax.ppermute only.
A program may use at most 32 MiB of HBM per device.

```python
import jax
import jax.numpy as jnp

TILE = 64
IJ = 4096
CDW = 3072
ABW = 98304


def set_ends(result, stream_key, low, high):
    longest = result.shape.index(max(result.shape))
    spots = []
    for shift in (0, 1):
        where = [jax.random.randint(jax.random.fold_in(stream_key, axis), (), 0, length) for axis, length in enumerate(result.shape)]
        where[longest] = (where[longest] + shift) % result.shape[longest]
        spots.append(tuple(where))
    return result.at[spots[0]].set(low).at[spots[1]].set(high)


def block_levels(rng, dims, cuts, least, top_value):
    loudness, own = 1.0, jax.random.fold_in(rng, 6)
    for position, parts in cuts:
        draws = jnp.exp(jax.random.uniform(jax.random.fold_in(own, position), (parts,), jnp.float32, least / len(cuts), top_value / len(cuts)))
        loudness = loudness * jnp.repeat(draws, dims[position] // parts).reshape([-1 if axis == position else 1 for axis in range(len(dims))])
    return loudness


def noise(rng, extent, deviation, reach, split=(), kind=jnp.bfloat16):
    result = deviation * jax.random.normal(rng, extent, jnp.float32)
    if split:
        result = result * block_levels(rng, extent, split, -0.22, 0.18)
    return jnp.clip(result, -reach, reach).astype(kind)


def setup_inputs(seed: int = 0) -> dict:
    key_of = jax.random.split(jax.random.key(seed), 5)
    return {
        "amplitudes": noise(key_of[0], (IJ, CDW), 1.0, 6.0, ((0, 8), (1, 96))),
        "integrals": noise(key_of[1], (CDW, ABW), CDW ** -0.5, 0.109375, ((0, 8), (1, 96))),
        "amp_mask": set_ends((jax.random.randint(key_of[2], (IJ // TILE, CDW // TILE), 0, 4) < 3).astype(jnp.int32), jax.random.fold_in(key_of[2], 1), 0, 1),
        "int_mask": set_ends((jax.random.randint(key_of[3], (CDW // TILE, ABW // TILE), 0, 4) < 3).astype(jnp.int32), jax.random.fold_in(key_of[3], 1), 0, 1),
    }


def expand(mask):
    return jnp.repeat(jnp.repeat(mask, TILE, axis=0), TILE, axis=1).astype(jnp.bfloat16)


def reference(amplitudes, integrals, amp_mask, int_mask):
    masked_amplitudes = amplitudes * expand(amp_mask)
    masked_integrals = integrals * expand(int_mask)
    ladder = jnp.dot(masked_amplitudes, masked_integrals, preferred_element_type=jnp.float32)
    return ladder.astype(jnp.bfloat16)
```

```python
import jax
import jax.numpy as jnp
from jax import lax
from jax.experimental import pallas as pl
from jax.experimental.pallas import tpu as pltpu
from jax.sharding import PartitionSpec as P

TILE = 64
Y, Z = 8, 12
FAR, NEAR = 2, 4
COLS = 256


def vir(y, z):
    return (y % Y) * Z + z % Z


Z_GROUPS = [[vir(y, z) for z in range(Z)] for y in range(Y)]
FAR_GROUPS = [[vir(near + NEAR * k, z) for k in range(FAR)] for near in range(NEAR) for z in range(Z)]


def spread(block, axis, groups):
    copies = jnp.broadcast_to(block[None], (len(groups[0]),) + block.shape)
    return lax.all_to_all(copies, axis, 0, 0, axis_index_groups=groups)


def shift_y(block, step):
    return lax.ppermute(block, "vir", [(vir(y, z), vir(y + step, z)) for y in range(Y) for z in range(Z)])


def screen_kernel(mask_ref, block_ref, out_ref):
    depth, cols = block_ref.shape
    tiles, tile_cols = mask_ref.shape
    across = lax.broadcasted_iota(jnp.int32, (tile_cols, cols), 1) // TILE
    spread_to = (across == lax.broadcasted_iota(jnp.int32, (tile_cols, cols), 0)).astype(jnp.float32)
    rows = jnp.dot(mask_ref[...].astype(jnp.float32), spread_to, preferred_element_type=jnp.float32).astype(jnp.bfloat16)
    for t in range(tiles):
        part = slice(t * TILE, (t + 1) * TILE)
        out_ref[part, :] = block_ref[part, :] * rows[t : t + 1, :]


def screen(block, mask):
    return pl.pallas_call(
        screen_kernel,
        out_shape=jax.ShapeDtypeStruct(block.shape, block.dtype),
        compiler_params=pltpu.CompilerParams(vmem_limit_bytes=40 * 1024 * 1024),
        cost_estimate=pl.CostEstimate(flops=block.size, bytes_accessed=4 * block.size, transcendentals=0),
    )(mask, block)


def product_kernel(offsets, has_acc, where, mask_ref, *refs):
    n = len(offsets)
    near = where[0]
    t_refs, refs = refs[: 2 * n], refs[2 * n :]
    v_refs, refs = refs[:n], refs[n:]
    acc_ref, refs = (refs[0], refs[1:]) if has_acc else (None, refs)
    out_ref, lhs, row_mask = refs
    some, far, r, rows = t_refs[0].shape
    zs = 2 * some
    depth = zs * far * r
    per = TILE // r

    @pl.when(pl.program_id(0) == 0)
    def _():
        tiles = mask_ref.shape[0]
        tile_of = lax.broadcasted_iota(jnp.int32, (tiles, rows), 1) // TILE
        spread_to = (tile_of == lax.broadcasted_iota(jnp.int32, (tiles, rows), 0)).astype(jnp.float32)
        row_mask[...] = lax.dot_general(
            mask_ref[...].astype(jnp.float32), spread_to, (((0,), (0,)), ((), ())), preferred_element_type=jnp.float32
        )
        for q, off in enumerate(offsets):
            residue = lax.rem(near + off, NEAR)
            blocks = []
            for f in range(far):
                for z in range(zs):
                    tile = (residue + NEAR * f) * (zs // per) + z // per
                    mask = row_mask[pl.ds(tile, 1), :].astype(jnp.bfloat16)
                    blocks.append(t_refs[2 * q + z // some][z % some, f] * mask)
            lhs[:, q * depth : (q + 1) * depth] = jnp.concatenate(blocks, axis=0).T

    rhs = jnp.concatenate([v[...].reshape(depth, -1) for v in v_refs], axis=0)
    total = jnp.dot(lhs[...], rhs, preferred_element_type=jnp.float32)
    if has_acc:
        total = total + acc_ref[...]
    out_ref[...] = total.astype(out_ref.dtype)


def product(where, offsets, ts, amp_mask, v, acc, dtype):
    n = len(offsets)
    some, far, r, rows = ts[0].shape
    cols = v.shape[-1]
    depth = 2 * some * far * r

    def strip(off):
        return pl.BlockSpec((far, 1, v.shape[2], COLS), lambda i, w: (0, lax.rem(w[0] + off, NEAR), 0, i))

    in_specs = [pl.BlockSpec(amp_mask.shape, lambda i, w: (0, 0))]
    in_specs += [pl.BlockSpec((some, far, r, rows), lambda i, w: (0, 0, 0, 0)) for _ in ts]
    in_specs += [strip(off) for off in offsets]
    operands = [amp_mask] + list(ts) + [v] * n
    if acc is not None:
        in_specs.append(pl.BlockSpec((rows, COLS), lambda i, w: (0, i)))
        operands.append(acc)
    return pl.pallas_call(
        lambda *refs: product_kernel(offsets, acc is not None, *refs),
        grid_spec=pltpu.PrefetchScalarGridSpec(
            num_scalar_prefetch=1,
            grid=(cols // COLS,),
            in_specs=in_specs,
            out_specs=pl.BlockSpec((rows, COLS), lambda i, w: (0, i)),
            scratch_shapes=[
                pltpu.VMEM((rows, n * depth), jnp.bfloat16),
                pltpu.VMEM((amp_mask.shape[1], rows), jnp.float32),
            ],
        ),
        out_shape=jax.ShapeDtypeStruct((rows, cols), dtype),
        compiler_params=pltpu.CompilerParams(vmem_limit_bytes=40 * 1024 * 1024),
        cost_estimate=pl.CostEstimate(
            flops=2 * rows * cols * n * depth,
            bytes_accessed=2 * n * depth * (rows + cols) + 4 * rows * cols,
            transcendentals=0,
        ),
    )(where, *operands)


def on_device(amplitudes, integrals, amp_mask, int_mask):
    depth, cols = integrals.shape
    near = lax.rem(lax.axis_index("vir") // Z, NEAR)
    where = near[None].astype(jnp.int32)

    pair = spread(amplitudes.T, "vir", FAR_GROUPS)
    pair, integrals = lax.optimization_barrier((pair, integrals))
    v = lax.all_gather(screen(integrals, int_mask), "occ", axis=0)
    w = lax.all_gather(pair, "vir", axis=0, axis_index_groups=Z_GROUPS)
    w_a, w_b = w[: Z // 2], w[Z // 2 :]
    below_a = shift_y(w_a, 1)
    above_b = shift_y(w_b, -1)
    below_b = shift_y(w_b, 1)
    above_a = shift_y(w_a, -1)
    two_a = shift_y(below_a, 1)
    two_b = shift_y(above_b, -1)

    v = v.reshape(FAR, NEAR, depth, cols)
    acc = product(where, (0,), (w_a, w_b), amp_mask, v, None, jnp.float32)
    acc = product(where, (1, 3), (above_a, above_b, below_a, below_b), amp_mask, v, acc, jnp.float32)
    return product(where, (2,), (two_a, two_b), amp_mask, v, acc, jnp.bfloat16)


def solution(mesh):
    return jax.shard_map(
        on_device,
        mesh=mesh,
        in_specs=(P("occ", "vir"), P("occ", "vir"), P("occ", None), P("occ", "vir")),
        out_specs=P("occ", "vir"),
        check_vma=False,
    )
```

```python
import jax
import jax.numpy as jnp
from jax import lax
from jax.experimental import pallas as pl
from jax.experimental.pallas import tpu as pltpu
from jax.sharding import PartitionSpec as P

TILE = 64
X, CORES, Y, Z = 4, 2, 8, 12
FAR, NEAR = 2, 4
PARTS = 1
VMEM_LIMIT = 20 * 1024 * 1024
HINT = 10**11
SCREEN_VMEM_LIMIT = 60 * 1024 * 1024


def vir(y, z):
    return (y % Y) * Z + z % Z


def occ(x, c):
    return (x % X) * CORES + c


X_GROUPS = [[occ(x, c) for x in range(X)] for c in range(CORES)]
Z_GROUPS = [[vir(y, z) for z in range(Z)] for y in range(Y)]


def shift_y(block, step):
    return lax.ppermute(block, "vir", [(vir(y, z), vir(y + step, z)) for y in range(Y) for z in range(Z)])


def swap_cores(block):
    return lax.ppermute(block, "occ", [(occ(x, c), occ(x, 1 - c)) for x in range(X) for c in range(CORES)])


def after(block, other, flops=0):
    hold = pl.BlockSpec(memory_space=pl.ANY)
    return pl.pallas_call(
        lambda block_ref, other_ref, out_ref: None,
        in_specs=[hold, hold],
        out_specs=hold,
        out_shape=jax.ShapeDtypeStruct(block.shape, block.dtype),
        input_output_aliases={0: 0},
        compiler_params=pltpu.CompilerParams(vmem_limit_bytes=1024 * 1024),
        cost_estimate=pl.CostEstimate(flops=flops, bytes_accessed=0, transcendentals=0),
    )(block, other)


def screen_kernel(mask_ref, block_ref, out_ref, loaded, masked, in_sems, out_sems):
    depth, cols = loaded.shape
    tiles, tile_cols = mask_ref.shape
    copies = out_ref.shape[0]
    part = depth // PARTS
    cuts = [pl.ds(p * part, part) for p in range(PARTS)]
    loads = [pltpu.make_async_copy(block_ref.at[cut, :], loaded.at[cut, :], in_sems.at[p]) for p, cut in enumerate(cuts)]
    for load in loads:
        load.start()
    across = lax.broadcasted_iota(jnp.int32, (tile_cols, cols), 1) // TILE
    spread_to = (across == lax.broadcasted_iota(jnp.int32, (tile_cols, cols), 0)).astype(jnp.float32)
    rows = jnp.dot(mask_ref[...].astype(jnp.float32), spread_to, preferred_element_type=jnp.float32).astype(jnp.bfloat16)
    stores = []
    for p, cut in enumerate(cuts):
        loads[p].wait()
        for t in range(p * tiles // PARTS, (p + 1) * tiles // PARTS):
            at = slice(t * TILE, (t + 1) * TILE)
            masked[at, :] = loaded[at, :] * rows[t : t + 1, :]
        for k in range(copies):
            sem = out_sems.at[p * copies + k]
            stores.append(pltpu.make_async_copy(masked.at[cut, :], out_ref.at[k, cut, :], sem))
            stores[-1].start()
    for store in stores:
        store.wait()


def screen(block, mask, copies):
    hold = pl.BlockSpec(memory_space=pl.ANY)
    return pl.pallas_call(
        screen_kernel,
        in_specs=[pl.BlockSpec(memory_space=pltpu.VMEM), hold],
        out_specs=hold,
        out_shape=jax.ShapeDtypeStruct((copies,) + block.shape, block.dtype),
        scratch_shapes=[
            pltpu.VMEM(block.shape, block.dtype),
            pltpu.VMEM(block.shape, block.dtype),
            pltpu.SemaphoreType.DMA((PARTS,)),
            pltpu.SemaphoreType.DMA((PARTS * copies,)),
        ],
        compiler_params=pltpu.CompilerParams(vmem_limit_bytes=SCREEN_VMEM_LIMIT),
        cost_estimate=pl.CostEstimate(flops=block.size, bytes_accessed=8 * block.size, transcendentals=0),
    )(mask, block)


def product_kernel(origins, has_acc, strips, where, mask_ref, *refs):
    n = len(origins)
    t_refs, refs = refs[: 2 * n], refs[2 * n :]
    own_ref, mate_ref, refs = refs[0], refs[1], refs[2:]
    acc_ref, refs = (refs[0], refs[1:]) if has_acc else (None, refs)
    out_ref, lhs, rhs, row_mask, block, v_sems, out_sems = refs
    some, far, r, rows = t_refs[0].shape
    zs = 2 * some
    cd = zs * r
    per = TILE // r
    wide = out_ref.shape[1] // strips

    def fetch(v_ref, s, q, f):
        y = lax.rem(where[0] + origins[q][0] + NEAR * f, Y)
        k = q * far + f
        source = v_ref.at[y // CORES, :, pl.ds(s * wide, wide)]
        return pltpu.make_async_copy(source, rhs.at[s, pl.ds(k * cd, cd), :], v_sems.at[s * n * far + k])

    for s in range(strips):
        for q in range(n):
            mine = lax.rem(where[0] + origins[q][0], CORES) == where[1]
            for f in range(far):
                pl.when(mine)(lambda: fetch(own_ref, s, q, f).start())
                pl.when(jnp.logical_not(mine))(lambda: fetch(mate_ref, s, q, f).start())

    tiles = mask_ref.shape[1]
    tile_of = lax.broadcasted_iota(jnp.int32, (mask_ref.shape[0], rows), 1) // TILE
    spread_to = (tile_of == lax.broadcasted_iota(jnp.int32, (mask_ref.shape[0], rows), 0)).astype(jnp.float32)
    row_mask[...] = lax.dot_general(
        mask_ref[...].astype(jnp.float32), spread_to, (((0,), (0,)), ((), ())), preferred_element_type=jnp.float32
    )
    for q, halves in enumerate(origins):
        for f in range(far):
            y = lax.rem(where[0] + halves[0] + NEAR * f, Y)
            for z in range(zs):
                half = z // some
                slot = (f + (halves[half] - halves[0]) // NEAR) % far
                mask = row_mask[pl.ds(y * (tiles // Y) + z // per, 1), :].astype(jnp.bfloat16)
                at = (q * far + f) * cd + z * r
                lhs[at : at + r, :] = t_refs[2 * q + half][z % some, slot] * mask

    stores = []
    for s in range(strips):
        for q in range(n):
            for f in range(far):
                fetch(own_ref, s, q, f).wait()
        total = lax.dot_general(lhs[...], rhs[s], (((0,), (0,)), ((), ())), preferred_element_type=jnp.float32)
        if not has_acc:
            out_ref[:, s * wide : (s + 1) * wide] = total
            continue
        block[s] = (total + acc_ref[:, s * wide : (s + 1) * wide]).astype(block.dtype)
        stores.append(pltpu.make_async_copy(block.at[s], out_ref.at[:, pl.ds(s * wide, wide)], out_sems.at[s]))
        stores[-1].start()
    for store in stores:
        store.wait()


def product(where, origins, ts, amp_mask, v_own, v_mate, acc, strips):
    n = len(origins)
    some, far, r, rows = ts[0].shape
    cols = v_own.shape[-1]
    depth = n * 2 * some * far * r
    last = acc is not None
    whole = pl.BlockSpec(memory_space=pltpu.VMEM)
    hold = pl.BlockSpec(memory_space=pl.ANY)
    operands = [where, amp_mask] + list(ts) + [v_own, v_mate] + ([acc] if last else [])
    in_specs = [pl.BlockSpec(memory_space=pltpu.SMEM)] + [whole] * (1 + 2 * n) + [hold] * 2
    dtype = jnp.bfloat16 if last else jnp.float32
    return pl.pallas_call(
        lambda *refs: product_kernel(origins, last, strips, *refs),
        in_specs=in_specs + ([whole] if last else []),
        out_specs=hold if last else whole,
        scratch_shapes=[
            pltpu.VMEM((depth, rows), jnp.bfloat16),
            pltpu.VMEM((strips, depth, cols // strips), jnp.bfloat16),
            pltpu.VMEM((amp_mask.shape[1], rows), jnp.float32),
            pltpu.VMEM((strips, rows, cols // strips) if last else (8, 128), jnp.bfloat16),
            pltpu.SemaphoreType.DMA((strips * n * far,)),
            pltpu.SemaphoreType.DMA((strips,)),
        ],
        out_shape=jax.ShapeDtypeStruct((rows, cols), dtype),
        compiler_params=pltpu.CompilerParams(vmem_limit_bytes=VMEM_LIMIT),
        cost_estimate=pl.CostEstimate(
            flops=2 * rows * cols * depth, bytes_accessed=2 * depth * (rows + cols) + 4 * rows * cols, transcendentals=0
        ),
    )(*operands)


def on_device(amplitudes, integrals, amp_mask, int_mask):
    core = lax.rem(lax.axis_index("occ"), CORES)
    where = jnp.stack([lax.axis_index("vir") // Z, core]).astype(jnp.int32)

    t = amplitudes.T
    other = after(shift_y(t, NEAR), t, flops=HINT)
    v_own = lax.all_to_all(screen(integrals, int_mask, X), "occ", 0, 0, axis_index_groups=X_GROUPS)

    w = lax.all_gather(jnp.stack([t, other]), "vir", axis=0, axis_index_groups=Z_GROUPS)
    v_own = after(v_own, w[0, 0, :16])
    v_mate = swap_cores(v_own)
    w_a, w_b = w[: Z // 2], w[Z // 2 :]
    below_a = shift_y(w_a, 1)
    above_b = shift_y(w_b, -1)
    below_b = shift_y(w_b, 1)
    above_a = after(shift_y(w_a, -1), w[0, 0, :16], flops=HINT)
    two_a = shift_y(below_a, 1)
    two_b = shift_y(above_b, -1)

    ts = (w_a, w_b, above_a, above_b, below_a, below_b)
    acc = product(where, ((0, 0), (1, 1), (Y - 1, Y - 1)), ts, amp_mask, v_own, v_mate, None, 1)
    return product(where, ((Y - 2, 2),), (two_a, two_b), amp_mask, v_own, v_mate, acc, 2)


def solution(mesh):
    return jax.shard_map(
        on_device,
        mesh=mesh,
        in_specs=(P("occ", "vir"), P("occ", "vir"), P("occ", None), P("occ", "vir")),
        out_specs=P("occ", "vir"),
        check_vma=False,
    )
```

```python
import jax
import jax.numpy as jnp
from jax import lax
from jax.experimental import pallas as pl
from jax.experimental.pallas import tpu as pltpu
from jax.sharding import PartitionSpec as P

TILE = 64
X, CORES, Y, Z = 4, 2, 8, 12
FAR, NEAR = 2, 4
STRIPS = 2
VMEM_LIMIT = 20 * 1024 * 1024
HINT = 10**11
SCREEN_VMEM_LIMIT = 60 * 1024 * 1024


def vir(y, z):
    return (y % Y) * Z + z % Z


def occ(x, c):
    return (x % X) * CORES + c


X_GROUPS = [[occ(x, c) for x in range(X)] for c in range(CORES)]
Z_GROUPS = [[vir(y, z) for z in range(Z)] for y in range(Y)]


def shift_y(block, step):
    return lax.ppermute(block, "vir", [(vir(y, z), vir(y + step, z)) for y in range(Y) for z in range(Z)])


def swap_cores(block):
    return lax.ppermute(block, "occ", [(occ(x, c), occ(x, 1 - c)) for x in range(X) for c in range(CORES)])


def after(block, other, flops=0):
    hold = pl.BlockSpec(memory_space=pl.ANY)
    return pl.pallas_call(
        lambda block_ref, other_ref, out_ref: None,
        in_specs=[hold, hold],
        out_specs=hold,
        out_shape=jax.ShapeDtypeStruct(block.shape, block.dtype),
        input_output_aliases={0: 0},
        compiler_params=pltpu.CompilerParams(vmem_limit_bytes=1024 * 1024),
        cost_estimate=pl.CostEstimate(flops=flops, bytes_accessed=0, transcendentals=0),
    )(block, other)


def screen_kernel(mask_ref, block_ref, out_ref, masked, sems):
    depth, cols = block_ref.shape
    tiles, tile_cols = mask_ref.shape
    across = lax.broadcasted_iota(jnp.int32, (tile_cols, cols), 1) // TILE
    spread_to = (across == lax.broadcasted_iota(jnp.int32, (tile_cols, cols), 0)).astype(jnp.float32)
    rows = jnp.dot(mask_ref[...].astype(jnp.float32), spread_to, preferred_element_type=jnp.float32).astype(jnp.bfloat16)
    for t in range(tiles):
        part = slice(t * TILE, (t + 1) * TILE)
        masked[part, :] = block_ref[part, :] * rows[t : t + 1, :]
    copies = [pltpu.make_async_copy(masked, out_ref.at[k], sems.at[k]) for k in range(out_ref.shape[0])]
    for copy in copies:
        copy.start()
    for copy in copies:
        copy.wait()


def screen(block, mask, copies):
    whole = pl.BlockSpec(memory_space=pltpu.VMEM)
    return pl.pallas_call(
        screen_kernel,
        in_specs=[whole, whole],
        out_specs=pl.BlockSpec(memory_space=pl.ANY),
        out_shape=jax.ShapeDtypeStruct((copies,) + block.shape, block.dtype),
        scratch_shapes=[pltpu.VMEM(block.shape, block.dtype), pltpu.SemaphoreType.DMA((copies,))],
        compiler_params=pltpu.CompilerParams(vmem_limit_bytes=SCREEN_VMEM_LIMIT),
        cost_estimate=pl.CostEstimate(flops=block.size, bytes_accessed=8 * block.size, transcendentals=0),
    )(mask, block)


def spread_mask(mask_ref, row_mask):
    tile_of = lax.broadcasted_iota(jnp.int32, (mask_ref.shape[0], row_mask.shape[1]), 1) // TILE
    spread_to = (tile_of == lax.broadcasted_iota(jnp.int32, tile_of.shape, 0)).astype(jnp.float32)
    row_mask[...] = lax.dot_general(
        mask_ref[...].astype(jnp.float32), spread_to, (((0,), (0,)), ((), ())), preferred_element_type=jnp.float32
    )


def load_t(t_refs, loaded, sems):
    copies = [pltpu.make_async_copy(t, loaded.at[i], sems.at[i]) for i, t in enumerate(t_refs)]
    for copy in copies:
        copy.start()
    return copies


def screen_t(halves, q, copies, loaded, row_mask, lhs):
    some, far, r = loaded.shape[1:4]
    cd = 2 * some * r
    tiles = row_mask.shape[0]
    here = lax.axis_index("vir") // Z
    for half in range(2):
        copies[2 * q + half].wait()
        for f in range(far):
            y = lax.rem(here + halves[0] + NEAR * f, Y)
            slot = (f + (halves[half] - halves[0]) // NEAR) % FAR
            for z in range(some):
                tile = y * (tiles // Y) + (half * some + z) // (TILE // r)
                mask = row_mask[pl.ds(tile, 1), :].astype(jnp.bfloat16)
                at = (q * far + f) * cd + (half * some + z) * r
                lhs[at : at + r, :] = loaded[2 * q + half, z, slot] * mask


def fetch_v(offset, own_ref, mate_ref, target, sem, go):
    y = lax.rem(lax.axis_index("vir") // Z + offset, Y)
    mine = lax.rem(y, CORES) == lax.rem(lax.axis_index("occ"), CORES)
    if go:
        pl.when(mine)(lambda: pltpu.make_async_copy(own_ref.at[y // CORES], target, sem).start())
        pl.when(jnp.logical_not(mine))(lambda: pltpu.make_async_copy(mate_ref.at[y // CORES], target, sem).start())
    else:
        pltpu.make_async_copy(own_ref.at[y // CORES], target, sem).wait()


def first_kernel(origins, after_these, mask_ref, *refs):
    n = len(origins)
    t_refs, refs = refs[: 2 * n], refs[2 * n :]
    own_ref, mate_ref, out_ref, later_ref, loaded, lhs, rhs, row_mask, t_sems, v_sems = refs
    cd = own_ref.shape[1]

    def fetches(go):
        for i, halves in enumerate(origins):
            for f in range(FAR):
                k = i * FAR + f
                fetch_v(halves[0] + NEAR * f, own_ref, mate_ref, rhs.at[pl.ds(k * cd, cd), :], v_sems.at[k], go)

    def later(go):
        for f in range(FAR):
            sem = v_sems.at[n * FAR + f]
            fetch_v(after_these + NEAR * f, own_ref, mate_ref, later_ref.at[pl.ds(f * cd, cd), :], sem, go)

    copies = load_t(t_refs, loaded, t_sems)
    fetches(True)
    later(True)
    spread_mask(mask_ref, row_mask)
    for q, halves in enumerate(origins):
        screen_t(halves, q, copies, loaded, row_mask, lhs)
    fetches(False)
    out_ref[...] = lax.dot_general(lhs[...], rhs[...], (((0,), (0,)), ((), ())), preferred_element_type=jnp.float32)
    later(False)


def last_kernel(halves, mask_ref, a_ref, b_ref, v_ref, acc_ref, out_ref, loaded, lhs, row_mask, block, t_sems, out_sems):
    copies = load_t((a_ref, b_ref), loaded, t_sems)
    spread_mask(mask_ref, row_mask)
    screen_t(halves, 0, copies, loaded, row_mask, lhs)
    strips = block.shape[0]
    wide = block.shape[2]
    stores = []
    for s in range(strips):
        columns = slice(s * wide, (s + 1) * wide)
        total = lax.dot_general(lhs[...], v_ref[:, columns], (((0,), (0,)), ((), ())), preferred_element_type=jnp.float32)
        block[s] = (total + acc_ref[:, columns]).astype(block.dtype)
        stores.append(pltpu.make_async_copy(block.at[s], out_ref.at[:, pl.ds(s * wide, wide)], out_sems.at[s]))
        stores[-1].start()
    for store in stores:
        store.wait()


WHOLE = pl.BlockSpec(memory_space=pltpu.VMEM)
HOLD = pl.BlockSpec(memory_space=pl.ANY)


def hint(rows, cols, depth):
    return pl.CostEstimate(
        flops=2 * rows * cols * depth, bytes_accessed=2 * depth * (rows + cols) + 4 * rows * cols, transcendentals=0
    )


def first_product(origins, after_these, ts, amp_mask, v_own, v_mate):
    n = len(origins)
    rows = ts[0].shape[-1]
    cd, cols = v_own.shape[1:]
    depth = n * FAR * cd
    return pl.pallas_call(
        lambda *refs: first_kernel(origins, after_these, *refs),
        in_specs=[WHOLE] + [HOLD] * (2 * n + 2),
        out_specs=(WHOLE, WHOLE),
        out_shape=(jax.ShapeDtypeStruct((rows, cols), jnp.float32), jax.ShapeDtypeStruct((FAR * cd, cols), v_own.dtype)),
        scratch_shapes=[
            pltpu.VMEM((2 * n,) + ts[0].shape, jnp.bfloat16),
            pltpu.VMEM((depth, rows), jnp.bfloat16),
            pltpu.VMEM((depth, cols), jnp.bfloat16),
            pltpu.VMEM((amp_mask.shape[1], rows), jnp.float32),
            pltpu.SemaphoreType.DMA((2 * n,)),
            pltpu.SemaphoreType.DMA(((n + 1) * FAR,)),
        ],
        compiler_params=pltpu.CompilerParams(vmem_limit_bytes=VMEM_LIMIT),
        cost_estimate=hint(rows, cols, depth),
    )(amp_mask, *ts, v_own, v_mate)


def last_product(halves, t_a, t_b, amp_mask, v, acc):
    rows, cols = acc.shape
    depth = v.shape[0]
    return pl.pallas_call(
        lambda *refs: last_kernel(halves, *refs),
        in_specs=[WHOLE, HOLD, HOLD, WHOLE, WHOLE],
        out_specs=HOLD,
        out_shape=jax.ShapeDtypeStruct((rows, cols), jnp.bfloat16),
        scratch_shapes=[
            pltpu.VMEM((2,) + t_a.shape, jnp.bfloat16),
            pltpu.VMEM((depth, rows), jnp.bfloat16),
            pltpu.VMEM((amp_mask.shape[1], rows), jnp.float32),
            pltpu.VMEM((STRIPS, rows, cols // STRIPS), jnp.bfloat16),
            pltpu.SemaphoreType.DMA((2,)),
            pltpu.SemaphoreType.DMA((STRIPS,)),
        ],
        compiler_params=pltpu.CompilerParams(vmem_limit_bytes=VMEM_LIMIT),
        cost_estimate=hint(rows, cols, depth),
    )(amp_mask, t_a, t_b, v, acc)


def on_device(amplitudes, integrals, amp_mask, int_mask):
    t = amplitudes.T
    other = after(shift_y(t, NEAR), t, flops=HINT)
    v_own = lax.all_to_all(screen(integrals, int_mask, X), "occ", 0, 0, axis_index_groups=X_GROUPS)

    w = lax.all_gather(jnp.stack([t, other]), "vir", axis=0, axis_index_groups=Z_GROUPS)
    w_a, w_b = w[: Z // 2], w[Z // 2 :]
    v_own = after(v_own, w_b)
    v_mate = swap_cores(v_own)
    below_a = shift_y(w_a, 1)
    above_b = shift_y(w_b, -1)
    below_b = shift_y(w_b, 1)
    above_a = after(shift_y(w_a, -1), w_b, flops=HINT)
    two_a = shift_y(below_a, 1)
    two_b = shift_y(above_b, -1)

    ts = (w_a, w_b, above_a, above_b, below_a, below_b)
    acc, v_two = first_product(((0, 0), (1, 1), (Y - 1, Y - 1)), Y - 2, ts, amp_mask, v_own, v_mate)
    return last_product((Y - 2, 2), two_a, two_b, amp_mask, v_two, acc)


def solution(mesh):
    return jax.shard_map(
        on_device,
        mesh=mesh,
        in_specs=(P("occ", "vir"), P("occ", "vir"), P("occ", None), P("occ", "vir")),
        out_specs=P("occ", "vir"),
        check_vma=False,
    )
```

```python
import jax
import jax.numpy as jnp
from jax import lax
from jax.experimental import pallas as pl
from jax.experimental.pallas import tpu as pltpu
from jax.sharding import PartitionSpec as P

TILE = 64
X, CORES, Y, Z = 4, 2, 8, 12
FAR, NEAR = 2, 4
STRIPS = 4
PARTS = 3
WHOLE = pl.BlockSpec(memory_space=pltpu.VMEM)
HOLD = pl.BlockSpec(memory_space=pl.ANY)
VMEM_LIMIT = 20 * 1024 * 1024
HINT = 10**11
SCREEN_VMEM_LIMIT = 60 * 1024 * 1024


def vir(y, z):
    return (y % Y) * Z + z % Z


def occ(x, c):
    return (x % X) * CORES + c


X_GROUPS = [[occ(x, c) for x in range(X)] for c in range(CORES)]
Z_GROUPS = [[vir(y, z) for z in range(Z)] for y in range(Y)]


def shift_y(block, step):
    return lax.ppermute(block, "vir", [(vir(y, z), vir(y + step, z)) for y in range(Y) for z in range(Z)])


def swap_cores(block):
    return lax.ppermute(block, "occ", [(occ(x, c), occ(x, 1 - c)) for x in range(X) for c in range(CORES)])


def after(block, other, flops=0):
    return pl.pallas_call(
        lambda block_ref, other_ref, out_ref: None,
        in_specs=[HOLD, HOLD],
        out_specs=HOLD,
        out_shape=jax.ShapeDtypeStruct(block.shape, block.dtype),
        input_output_aliases={0: 0},
        compiler_params=pltpu.CompilerParams(vmem_limit_bytes=1024 * 1024),
        cost_estimate=pl.CostEstimate(flops=flops, bytes_accessed=0, transcendentals=0),
    )(block, other)


def screen_kernel(mask_ref, block_ref, out_ref, mask, loaded, masked, in_sems, out_sems):
    depth, cols = loaded.shape
    tiles, tile_cols = mask.shape
    copies = out_ref.shape[0]
    part = depth // PARTS
    cuts = [pl.ds(p * part, part) for p in range(PARTS)]
    loads = [pltpu.make_async_copy(mask_ref, mask, in_sems.at[PARTS])]
    loads += [pltpu.make_async_copy(block_ref.at[cut, :], loaded.at[cut, :], in_sems.at[p]) for p, cut in enumerate(cuts)]
    for load in loads:
        load.start()
    across = lax.broadcasted_iota(jnp.int32, (tile_cols, cols), 1) // TILE
    spread_to = (across == lax.broadcasted_iota(jnp.int32, (tile_cols, cols), 0)).astype(jnp.float32)
    loads[0].wait()
    rows = jnp.dot(mask[...].astype(jnp.float32), spread_to, preferred_element_type=jnp.float32).astype(jnp.bfloat16)
    stores = []
    for p, cut in enumerate(cuts):
        loads[p + 1].wait()
        for t in range(p * tiles // PARTS, (p + 1) * tiles // PARTS):
            at = slice(t * TILE, (t + 1) * TILE)
            masked[at, :] = loaded[at, :] * rows[t : t + 1, :]
        for k in range(copies):
            sem = out_sems.at[p * copies + k]
            stores.append(pltpu.make_async_copy(masked.at[cut, :], out_ref.at[k, cut, :], sem))
            stores[-1].start()
    for store in stores:
        store.wait()


def screen(block, mask, copies):
    return pl.pallas_call(
        screen_kernel,
        in_specs=[HOLD, HOLD],
        out_specs=HOLD,
        out_shape=jax.ShapeDtypeStruct((copies,) + block.shape, block.dtype),
        scratch_shapes=[
            pltpu.VMEM(mask.shape, mask.dtype),
            pltpu.VMEM(block.shape, block.dtype),
            pltpu.VMEM(block.shape, block.dtype),
            pltpu.SemaphoreType.DMA((PARTS + 1,)),
            pltpu.SemaphoreType.DMA((PARTS * copies,)),
        ],
        compiler_params=pltpu.CompilerParams(vmem_limit_bytes=SCREEN_VMEM_LIMIT),
        cost_estimate=pl.CostEstimate(flops=block.size, bytes_accessed=8 * block.size, transcendentals=0),
    )(mask, block)


def spread_mask(mask_ref, row_mask):
    tile_of = lax.broadcasted_iota(jnp.int32, (mask_ref.shape[0], row_mask.shape[1]), 1) // TILE
    spread_to = (tile_of == lax.broadcasted_iota(jnp.int32, tile_of.shape, 0)).astype(jnp.float32)
    row_mask[...] = lax.dot_general(
        mask_ref[...].astype(jnp.float32), spread_to, (((0,), (0,)), ((), ())), preferred_element_type=jnp.float32
    )


def load_t(t_refs, loaded, sems):
    copies = [pltpu.make_async_copy(t, loaded.at[i], sems.at[i]) for i, t in enumerate(t_refs)]
    for copy in copies:
        copy.start()
    return copies


def screen_t(halves, q, copies, loaded, row_mask, lhs):
    some, far, r = loaded.shape[1:4]
    cd = 2 * some * r
    tiles = row_mask.shape[0]
    here = lax.axis_index("vir") // Z
    for half in range(2):
        copies[2 * q + half].wait()
        for f in range(far):
            y = lax.rem(here + halves[0] + NEAR * f, Y)
            slot = (f + (halves[half] - halves[0]) // NEAR) % FAR
            for z in range(some):
                tile = y * (tiles // Y) + (half * some + z) // (TILE // r)
                mask = row_mask[pl.ds(tile, 1), :].astype(jnp.bfloat16)
                at = (q * far + f) * cd + (half * some + z) * r
                lhs[at : at + r, :] = loaded[2 * q + half, z, slot] * mask


def fetch_v(offset, own_ref, mate_ref, target, sem, go):
    y = lax.rem(lax.axis_index("vir") // Z + offset, Y)
    mine = lax.rem(y, CORES) == lax.rem(lax.axis_index("occ"), CORES)
    if go:
        pl.when(mine)(lambda: pltpu.make_async_copy(own_ref.at[y // CORES], target, sem).start())
        pl.when(jnp.logical_not(mine))(lambda: pltpu.make_async_copy(mate_ref.at[y // CORES], target, sem).start())
    else:
        pltpu.make_async_copy(own_ref.at[y // CORES], target, sem).wait()


def rows_kernel(origins, mask_ref, *refs):
    n = len(origins)
    t_refs, refs = refs[: 2 * n], refs[2 * n :]
    out_ref, loaded, lhs, row_mask, t_sems = refs
    copies = load_t(t_refs, loaded, t_sems)
    spread_mask(mask_ref, row_mask)
    depth = lhs.shape[0]
    for q, halves in enumerate(origins):
        screen_t(halves, 0, copies[2 * q : 2 * q + 2], loaded.at[2 * q : 2 * q + 2], row_mask, lhs)
        out_ref[:, q * depth : (q + 1) * depth] = lhs[...].T


def first_kernel(origins, after_these, lhs_ref, own_ref, mate_ref, out_ref, later_ref, rhs, v_sems):
    n = len(origins)
    cd = own_ref.shape[1]

    def fetches(go):
        for i, halves in enumerate(origins):
            for f in range(FAR):
                k = i * FAR + f
                fetch_v(halves[0] + NEAR * f, own_ref, mate_ref, rhs.at[pl.ds(k * cd, cd), :], v_sems.at[k], go)

    def later(go):
        for f in range(FAR):
            sem = v_sems.at[n * FAR + f]
            fetch_v(after_these + NEAR * f, own_ref, mate_ref, later_ref.at[pl.ds(f * cd, cd), :], sem, go)

    fetches(True)
    later(True)
    fetches(False)
    out_ref[...] = jnp.dot(lhs_ref[...], rhs[...], preferred_element_type=jnp.float32)
    later(False)


def last_kernel(halves, mask_ref, a_ref, b_ref, v_ref, acc_ref, out_ref, loaded, rows, lhs, row_mask, block, t_sems, out_sems):
    copies = load_t((a_ref, b_ref), loaded, t_sems)
    spread_mask(mask_ref, row_mask)
    screen_t(halves, 0, copies, loaded, row_mask, rows)
    lhs[...] = rows[...].T
    strips = block.shape[0]
    wide = block.shape[2]
    stores = []
    for s in range(strips):
        columns = slice(s * wide, (s + 1) * wide)
        total = jnp.dot(lhs[...], v_ref[:, columns], preferred_element_type=jnp.float32)
        block[s] = (total + acc_ref[:, columns]).astype(block.dtype)
        stores.append(pltpu.make_async_copy(block.at[s], out_ref.at[:, pl.ds(s * wide, wide)], out_sems.at[s]))
        stores[-1].start()
    for store in stores:
        store.wait()


def hint(rows, cols, depth):
    return pl.CostEstimate(
        flops=2 * rows * cols * depth, bytes_accessed=2 * depth * (rows + cols) + 4 * rows * cols, transcendentals=0
    )


def masked_rows(origins, ts, amp_mask):
    n = len(origins)
    some, far, r, rows = ts[0].shape
    depth = 2 * some * far * r
    return pl.pallas_call(
        lambda *refs: rows_kernel(origins, *refs),
        in_specs=[WHOLE] + [HOLD] * (2 * n),
        out_specs=WHOLE,
        out_shape=jax.ShapeDtypeStruct((rows, n * depth), jnp.bfloat16),
        scratch_shapes=[
            pltpu.VMEM((2 * n,) + ts[0].shape, jnp.bfloat16),
            pltpu.VMEM((depth, rows), jnp.bfloat16),
            pltpu.VMEM((amp_mask.shape[1], rows), jnp.float32),
            pltpu.SemaphoreType.DMA((2 * n,)),
        ],
        compiler_params=pltpu.CompilerParams(vmem_limit_bytes=VMEM_LIMIT),
        cost_estimate=pl.CostEstimate(flops=rows * n * depth, bytes_accessed=4 * rows * n * depth, transcendentals=0),
    )(amp_mask, *ts)


def first_product(origins, after_these, lhs, v_own, v_mate):
    n = len(origins)
    rows, depth = lhs.shape
    cd, cols = v_own.shape[1:]
    return pl.pallas_call(
        lambda *refs: first_kernel(origins, after_these, *refs),
        in_specs=[WHOLE, HOLD, HOLD],
        out_specs=(WHOLE, WHOLE),
        out_shape=(jax.ShapeDtypeStruct((rows, cols), jnp.float32), jax.ShapeDtypeStruct((FAR * cd, cols), v_own.dtype)),
        scratch_shapes=[pltpu.VMEM((depth, cols), jnp.bfloat16), pltpu.SemaphoreType.DMA(((n + 1) * FAR,))],
        compiler_params=pltpu.CompilerParams(vmem_limit_bytes=VMEM_LIMIT),
        cost_estimate=hint(rows, cols, depth),
    )(lhs, v_own, v_mate)


def last_product(halves, t_a, t_b, amp_mask, v, acc):
    rows, cols = acc.shape
    depth = v.shape[0]
    return pl.pallas_call(
        lambda *refs: last_kernel(halves, *refs),
        in_specs=[WHOLE, HOLD, HOLD, WHOLE, WHOLE],
        out_specs=HOLD,
        out_shape=jax.ShapeDtypeStruct((rows, cols), jnp.bfloat16),
        scratch_shapes=[
            pltpu.VMEM((2,) + t_a.shape, jnp.bfloat16),
            pltpu.VMEM((depth, rows), jnp.bfloat16),
            pltpu.VMEM((rows, depth), jnp.bfloat16),
            pltpu.VMEM((amp_mask.shape[1], rows), jnp.float32),
            pltpu.VMEM((STRIPS, rows, cols // STRIPS), jnp.bfloat16),
            pltpu.SemaphoreType.DMA((2,)),
            pltpu.SemaphoreType.DMA((STRIPS,)),
        ],
        compiler_params=pltpu.CompilerParams(vmem_limit_bytes=VMEM_LIMIT),
        cost_estimate=hint(rows, cols, depth),
    )(amp_mask, t_a, t_b, v, acc)


def on_device(amplitudes, integrals, amp_mask, int_mask):
    t = amplitudes.T
    other = after(shift_y(t, NEAR), t, flops=HINT)
    v_own = lax.all_to_all(screen(integrals, int_mask, X), "occ", 0, 0, axis_index_groups=X_GROUPS)

    w = lax.all_gather(jnp.stack([t, other]), "vir", axis=0, axis_index_groups=Z_GROUPS)
    w_a, w_b = w[: Z // 2], w[Z // 2 :]
    v_own = after(v_own, w_b)
    v_mate = swap_cores(v_own)
    below_a = shift_y(w_a, 1)
    above_b = shift_y(w_b, -1)
    below_b = shift_y(w_b, 1)
    above_a = after(shift_y(w_a, -1), w_b, flops=HINT)
    two_a = shift_y(below_a, 1)
    two_b = shift_y(above_b, -1)

    ts = (w_a, w_b, above_a, above_b, below_a, below_b)
    origins = ((0, 0), (1, 1), (Y - 1, Y - 1))
    acc, v_two = first_product(origins, Y - 2, masked_rows(origins, ts, amp_mask), v_own, v_mate)
    return last_product((Y - 2, 2), two_a, two_b, amp_mask, v_two, acc)


def solution(mesh):
    return jax.shard_map(
        on_device,
        mesh=mesh,
        in_specs=(P("occ", "vir"), P("occ", "vir"), P("occ", None), P("occ", "vir")),
        out_specs=P("occ", "vir"),
        check_vma=False,
    )
```
